256 devices in a mesh: gx: 8 (over z_lo, core), gy: 8 (over x, z_hi), gz: 4 (over y).
Axes of the slice: x: 4, y: 4, z: 8 (z_hi: 2, z_lo: 4; z = z_hi * 4 + z_lo), core: 2. Of those that a mesh axis runs over, the one named last changes fastest.
Arguments:
- inputs: bfloat16 [2048, 8192], P('gx', ('gy', 'gz')), may hold values from -6 to 6
- hidden_grad: bfloat16 [2048, 14336], P(('gx', 'gy'), 'gz'), may hold values from -6 to 6
- gate_pre: bfloat16 [2048, 14336], P(('gx', 'gy'), 'gz'), may hold values from -8 to 8
- up_pre: bfloat16 [2048, 14336], P(('gx', 'gy'), 'gz'), may hold values from -6 to 6
- gate_weight: bfloat16 [8192, 14336], P(('gy', 'gx'), 'gz'), may hold values from -0.0625 to 0.0625
- up_weight: bfloat16 [8192, 14336], P(('gy', 'gx'), 'gz'), may hold values from -0.0625 to 0.0625
Outputs:
- input_grad: bfloat16 [2048, 8192], P('gx', ('gy', 'gz'))
- gate_weight_grad: bfloat16 [8192, 14336], P(('gy', 'gx'), 'gz')
- up_weight_grad: bfloat16 [8192, 14336], P(('gy', 'gx'), 'gz')
The draws below stay inside these ranges and needn't reach their ends.
All inputs are finite; a program needn't handle non-finite values.
Results may differ from the reference program's by a relative error of at most 0.019.
Values may be sent and summed in bfloat16 or wider, within the bound.
A program may use at most 128 MiB of HBM per device.

```python
import math
import jax
import jax.numpy as jnp
from jax import lax

D = 8192
FF = 14336
M_BLK = 256
TOKENS = 2048
N_GX = 8


def steps_of(rng, dims, cuts, low, largest):
    gain = 1.0
    for axis_at, blocks in cuts:
        draws = jax.random.uniform(jax.random.fold_in(jax.random.fold_in(rng, 6), axis_at), (blocks,), jnp.float32, low / len(cuts), largest / len(cuts))
        gain = gain * jnp.repeat(jnp.exp(draws), dims[axis_at] // blocks).reshape((-1,) + (1,) * (len(dims) - 1 - axis_at))
    return gain


def bell_draw(rng, dims, width, limit, cuts=(), dtype=jnp.bfloat16):
    values = width * jax.random.normal(rng, dims, jnp.float32)
    if cuts:
        values = values * steps_of(rng, dims, cuts, -0.22, 0.18)
    return jnp.clip(values, -limit, limit).astype(dtype)


def setup_inputs(seed: int = 0) -> dict:
    streams_of = jax.random.split(jax.random.key(seed), 7)
    inputs = bell_draw(streams_of[0], (TOKENS, D), 1.0, 6.0, ((0, 8), (1, 32)))
    hidden_grad = bell_draw(streams_of[1], (TOKENS, FF), 1.0, 6.0, ((0, 64), (1, 4)))
    gate_pre = bell_draw(streams_of[2], (TOKENS, FF), 1.5, 8.0, ((0, 64), (1, 4)))
    up_pre = bell_draw(streams_of[3], (TOKENS, FF), 1.0, 6.0, ((0, 64), (1, 4)))
    gate_weight = bell_draw(streams_of[4], (D, FF), D ** -0.5, 0.0625, ((0, 64), (1, 4)))
    up_weight = bell_draw(streams_of[5], (D, FF), D ** -0.5, 0.0625, ((0, 64), (1, 4)))
    return dict(inputs=inputs, hidden_grad=hidden_grad, gate_pre=gate_pre, up_pre=up_pre, gate_weight=gate_weight, up_weight=up_weight)


def hidden_terms(hidden_grad, gate_pre, up_pre):
    incoming = hidden_grad.astype(jnp.float32)
    gating = gate_pre.astype(jnp.float32)
    upper = up_pre.astype(jnp.float32)
    squash = jax.nn.sigmoid(gating)
    gate_grad = (incoming * upper * squash * (1.0 + gating * (1.0 - squash))).astype(jnp.bfloat16)
    up_grad = (incoming * gating * squash).astype(jnp.bfloat16)
    return (gate_grad, up_grad)

def reference(inputs, hidden_grad, gate_pre, up_pre, gate_weight, up_weight):
    gate_grad, up_grad = hidden_terms(hidden_grad, gate_pre, up_pre)
    backward = jnp.dot(gate_grad, gate_weight.T, preferred_element_type=jnp.float32)
    backward = backward + jnp.dot(up_grad, up_weight.T, preferred_element_type=jnp.float32)
    input_grad = backward.astype(jnp.bfloat16)
    input_blocks = inputs.reshape(N_GX, M_BLK, D)
    gate_blocks = gate_grad.reshape(N_GX, M_BLK, FF)
    up_blocks = up_grad.reshape(N_GX, M_BLK, FF)

    def accumulate(carry, items):
        token_rows, gate_part, up_part = items
        first = jnp.dot(token_rows.T, gate_part, preferred_element_type=jnp.float32)
        second = jnp.dot(token_rows.T, up_part, preferred_element_type=jnp.float32)
        first = first.astype(jnp.bfloat16).astype(jnp.float32)
        second = second.astype(jnp.bfloat16).astype(jnp.float32)
        return ((carry[0] + first, carry[1] + second), None)
    start = (jnp.zeros((D, FF), jnp.float32), jnp.zeros((D, FF), jnp.float32))
    totals, unused = lax.scan(accumulate, start, (input_blocks, gate_blocks, up_blocks))
    factor = 1.0 / math.sqrt(TOKENS)
    gate_weight_grad = (totals[0] * factor).astype(jnp.bfloat16)
    up_weight_grad = (totals[1] * factor).astype(jnp.bfloat16)
    return (input_grad, gate_weight_grad, up_weight_grad)
```

```python
import functools
import math

import jax
import jax.numpy as jnp
from jax import lax
from jax.experimental import pallas as pl
from jax.experimental.pallas import tpu as pltpu
from jax.sharding import PartitionSpec as P

MESH = pl.DeviceIdType.MESH
BF16, F32 = jnp.bfloat16, jnp.float32

NX, NY, NZH, NZL = 4, 4, 2, 4
NZ = NZH * NZL


def aligned(index, step, size):
    return pl.ds(pl.multiple_of(index * step, step), size)


def kernel(
    factor,
    x_ref, h_ref, g_ref, u_ref, wg_ref, wu_ref,
    dx_ref, dwg_ref, dwu_ref,
    g0, gbuf, wbuf, xt0, xbuf, dxs, dxr, dxp, dxq, dwt, dws, dwr, dwf,
    ga_s, ga_r, gr_s, gr_r, wa_s, wa_r, wc_s, wc_r, xa_s, xa_r, xb_s, xb_r,
    dy_s, dy_r, dq_s, dq_r, ec_s, ec_r, eo_s, eo_r,
):
    gx, gy, gz = lax.axis_index("gx"), lax.axis_index("gy"), lax.axis_index("gz")
    x, zh, y, zl, c = gy // NZH, gy % NZH, gz, gx // 2, gx % 2
    z = zh * NZL + zl
    rows = h_ref.shape[0]
    fq = h_ref.shape[1] // NX
    wr = wg_ref.shape[0]
    dc = 2 * wr
    shard = NX * rows
    blk = NZH * shard
    half = shard // 2
    w_refs, dw_refs = (wg_ref, wu_ref), (dwg_ref, dwu_ref)

    def dev(xx, yy, zz, cc):
        return ((zz % NZL) * 2 + cc, xx * NZH + zz // NZL, yy)

    def remote(src, dst, ss, rs, to):
        return pltpu.make_async_remote_copy(
            src_ref=src, dst_ref=dst, send_sem=ss, recv_sem=rs, device_id=to, device_id_type=MESH
        )

    here = dev(x, y, z, c)
    pair = dev(x, y, z, 1 - c)
    xs = [(x + k) % NX for k in range(NX)]
    ys = [(y + k) % NY for k in range(NY)]
    up, down = dev(x, y, (z + 1) % NZ, c), dev(x, y, (z + NZ - 1) % NZ, c)
    swapped = [dev(xs[k], zl, zh * NZL + y, c) for k in range(NX)]
    on_diag = y == zl

    def landed(ref, sem):
        remote(ref, ref, sem, sem, pair).wait_recv()

    def sent(ref, sem):
        remote(ref, ref, sem, sem, pair).wait_send()

    barrier = pltpu.get_barrier_semaphore()

    def greet(to):
        pl.semaphore_signal(barrier, inc=1, device_id=to, device_id_type=MESH)

    for k in range(1, NX):
        greet(dev(xs[k], y, z, c))
    for k in range(1, NY):
        greet(dev(x, ys[k], z, c))
    greet(up)
    greet(down)
    greet(pair)

    @pl.when(on_diag)
    def _():
        pl.semaphore_wait(barrier, (NX - 1) + (NY - 1) + 3)

    @pl.when(jnp.logical_not(on_diag))
    def _():
        for k in range(NX):
            greet(swapped[k])
        pl.semaphore_wait(barrier, (NX - 1) + (NY - 1) + 3 + NX)

    for q in range(NX):
        part = slice(q * fq, (q + 1) * fq)
        hh = h_ref[:, part].astype(F32)
        gg = g_ref[:, part].astype(F32)
        uu = u_ref[:, part].astype(F32)
        sq = jax.nn.sigmoid(gg)
        g0[q, 0] = (hh * uu * sq * (1.0 + gg * (1.0 - sq))).astype(BF16)
        g0[q, 1] = (hh * gg * sq).astype(BF16)

    def place(zz):
        zz = zz % NZ
        return (zz % NZL) * NZH + zz // NZL

    mine = place(z)
    g_mine = gbuf.at[:, mine, aligned(x, rows, rows), :]
    pltpu.make_async_copy(g0.at[x], g_mine, ga_r.at[x]).start()
    for k in range(1, NX):
        remote(g0.at[xs[k]], g_mine, ga_s.at[k], ga_r.at[x], dev(xs[k], y, z, c)).start()

    xin = x_ref[...].astype(F32)
    xp = jnp.concatenate(
        [xin[(i * NZH + j) * rows:(i * NZH + j + 1) * rows] for j in range(NZH) for i in range(NX)], axis=0
    )
    xt0[...] = xp.T.astype(BF16)
    x_dst = xbuf.at[aligned(x, dc, dc), aligned(zl, blk, blk)]

    def x_send(k):
        return remote(xt0, x_dst, xa_s.at[k], xa_r.at[x], swapped[k])

    for k in range(1, NX):
        x_send(k).start()

    @pl.when(on_diag)
    def _():
        pltpu.make_async_copy(xt0, x_dst, xa_r.at[x]).start()

    @pl.when(jnp.logical_not(on_diag))
    def _():
        x_send(0).start()

    def w_src(gu, q):
        return w_refs[gu].at[:, aligned(q, fq, fq)]

    def w_rows(gu, i, cc):
        return wbuf.at[gu, aligned(i * 2 + cc, wr, wr), :]

    def w_send(gu, k):
        return remote(w_src(gu, xs[k]), w_rows(gu, x, c), wa_s.at[gu, k], wa_r.at[gu, x], dev(xs[k], y, z, c))

    for gu in range(2):
        pltpu.make_async_copy(w_src(gu, x), w_rows(gu, x, c), wa_r.at[gu, x]).start()
        for k in range(1, NX):
            w_send(gu, k).start()

    def w_forward(gu):
        for i in range(NX):
            landed(w_rows(gu, i, c), wa_r.at[gu, i])
            remote(w_rows(gu, i, c), w_rows(gu, i, c), wc_s.at[gu, i], wc_r.at[gu, i], pair).start()

    def ring_ref(gu, zz, part):
        return gbuf.at[gu, place(zz), pl.ds(part * half, half), :]

    def ring_send(gu, d, s, part):
        ref = ring_ref(gu, z + (NZ - s if d == 0 else s), part)
        return remote(ref, ref, gr_s.at[gu, d, s, part], gr_r.at[gu, d, s, part], up if d == 0 else down)

    def ring_landed(gu, d, s, part):
        landed(ring_ref(gu, z + (NZ - 1 - s if d == 0 else 1 + s), part), gr_r.at[gu, d, s, part])

    def part_of(d, j):
        return j if d == 0 else 1 - j

    last = NZ // 2 - 1

    def ring_first(gu):
        for j in range(2):
            for d in range(2):
                ring_send(gu, d, 0, part_of(d, j)).start()

    def ring_step(gu, s):
        for j in range(2 if s < last else 1):
            for d in range(2):
                ring_landed(gu, d, s - 1, part_of(d, j))
                ring_send(gu, d, s, part_of(d, j)).start()

    def ring_end(gu):
        for d in range(2):
            ring_landed(gu, d, last - 1, part_of(d, 1))
        for d in range(2):
            ring_landed(gu, d, last, part_of(d, 0))

    for i in range(NX):
        landed(gbuf.at[:, mine, pl.ds(i * rows, rows), :], ga_r.at[i])
    ring_first(0)

    for i in range(NX):
        landed(xbuf.at[pl.ds(i * dc, dc), aligned(y, blk, blk)], xa_r.at[i])
    x_block = xbuf.at[:, aligned(y, blk, blk)]
    for k in range(1, NY):
        remote(x_block, x_block, xb_s.at[k], xb_r.at[y], dev(x, ys[k], z, c)).start()

    ring_step(0, 1)
    w_forward(0)
    ring_step(0, 2)
    ring_step(0, 3)
    ring_first(1)
    w_forward(1)

    def dw_out(gu, q):
        return dw_refs[gu].at[:, aligned(q, fq, fq)]

    def dw_send(gu, k):
        return remote(dwf.at[gu, xs[k]], dw_out(gu, x), eo_s.at[gu, k], eo_r.at[gu, x], dev(xs[k], y, z, c))

    def dw_pair(gu, i):
        return remote(dws.at[gu, i], dwr.at[gu, i], ec_s.at[gu, i], ec_r.at[gu, i], pair)

    def dw_compute(gu):
        tokens = gbuf.at[gu]

        @pl.loop(0, NX)
        def _(i):
            lhs = xbuf[aligned(i, dc, dc), :]
            rhs = tokens[...].reshape(NZ * shard, fq)
            dwt[gu, i] = jnp.dot(lhs, rhs, preferred_element_type=F32)
            dws[gu, i] = dwt[gu, i, aligned(1 - c, wr, wr), :].astype(BF16)
            dw_pair(gu, i).start()

    def dw_finish(gu):
        for k in range(NX - 1, -1, -1):
            i = xs[k]
            landed(dwr.at[gu, i], ec_r.at[gu, i])
            total = dwt[gu, i, aligned(c, wr, wr), :] + dwr[gu, i].astype(F32)
            dwf[gu, i] = (total * factor).astype(BF16)
            if k:
                dw_send(gu, k).start()
            else:
                pltpu.make_async_copy(dwf.at[gu, i], dw_out(gu, x), eo_r.at[gu, x]).start()

    def dx_parts(p, d_zh, d_zl):
        return dxs.at[p], dxr.at[y, d_zh]

    def dx_shard(zz):
        zz = zz % NZ
        p, j, owner = place(zz), zz // NZL, zz % NZL

        @pl.loop(0, NX)
        def _(i):
            columns = aligned(i, dc, dc)
            total = lax.dot_general(
                gbuf[0, p], wbuf[0, columns, :], (((1,), (1,)), ((), ())), preferred_element_type=F32
            ) + lax.dot_general(
                gbuf[1, p], wbuf[1, columns, :], (((1,), (1,)), ((), ())), preferred_element_type=F32
            )
            dxs[p, :, columns] = total.astype(BF16)

        @pl.when(owner == y)
        def _():
            pltpu.make_async_copy(dxs.at[p], dxr.at[y, j], dy_r.at[y, j]).start()

        @pl.when(owner != y)
        def _():
            remote(dxs.at[p], dxr.at[y, j], dy_s.at[p], dy_r.at[y, j], dev(x, owner, z, c)).start()

    ring_end(0)
    for k in range(1, NY):
        landed(xbuf.at[:, aligned(ys[k], blk, blk)], xb_r.at[ys[k]])
    dw_compute(0)
    ring_step(1, 1)
    dw_finish(0)
    for gu in range(2):
        for i in range(NX):
            landed(w_rows(gu, i, 1 - c), wc_r.at[gu, i])
    dx_shard(z)
    ring_step(1, 2)
    dx_shard(z + NZ - 1)
    dx_shard(z + 1)
    ring_step(1, 3)
    dx_shard(z + NZ - 2)
    dx_shard(z + 2)
    ring_end(1)
    dx_shard(z + NZ - 3)
    dx_shard(z + 3)
    dx_shard(z + 4)
    dw_compute(1)
    dw_finish(1)

    for i in range(NY):
        for j in range(NZH):
            landed(dxr.at[i, j], dy_r.at[i, j])
    for i in range(NX):
        columns = slice(i * dc, (i + 1) * dc)
        total = dxr[0, :, :, columns].astype(F32)
        for k in range(1, NY):
            total = total + dxr[k, :, :, columns].astype(F32)
        dxp[i] = total.astype(BF16)

    def dx_send(k):
        return remote(dxp.at[xs[k]], dxq.at[x], dq_s.at[k], dq_r.at[x], swapped[k])

    for k in range(1, NX):
        dx_send(k).start()

    @pl.when(on_diag)
    def _():
        pltpu.make_async_copy(dxp.at[x], dxq.at[x], dq_r.at[x]).start()

    @pl.when(jnp.logical_not(on_diag))
    def _():
        dx_send(0).start()

    for i in range(NX):
        landed(dxq.at[i], dq_r.at[i])
    for j in range(NZH):
        for i in range(NX):
            part = slice(i * rows, (i + 1) * rows)
            total = dxq[0, j, part, :].astype(F32)
            for k in range(1, NX):
                total = total + dxq[k, j, part, :].astype(F32)
            dx_ref[(i * NZH + j) * rows:(i * NZH + j + 1) * rows, :] = total.astype(BF16)

    for gu in range(2):
        for i in range(NX):
            landed(dw_out(gu, i), eo_r.at[gu, i])
    for k in range(1, NX):
        sent(g0.at[xs[k]], ga_s.at[k])
        sent(xt0, xa_s.at[k])
        sent(x_block, xb_s.at[k])
        sent(dxp.at[xs[k]], dq_s.at[k])
        for gu in range(2):
            sent(w_src(gu, xs[k]), wa_s.at[gu, k])
            sent(dwf.at[gu, xs[k]], eo_s.at[gu, k])

    @pl.when(jnp.logical_not(on_diag))
    def _():
        sent(xt0, xa_s.at[0])
        sent(dxp.at[x], dq_s.at[0])

    for gu in range(2):
        for i in range(NX):
            sent(w_rows(gu, i, c), wc_s.at[gu, i])
            sent(dws.at[gu, i], ec_s.at[gu, i])
        for s in range(last + 1):
            for j in range(2 if s < last else 1):
                for d in range(2):
                    ring_send(gu, d, s, part_of(d, j)).wait_send()
    for p in range(NZ):

        @pl.when(p // NZH != y)
        def _():
            sent(dxs.at[p], dy_s.at[p])


def body(inputs, hidden_grad, gate_pre, up_pre, gate_weight, up_weight):
    rows, width = hidden_grad.shape
    wr = gate_weight.shape[0]
    fq, shard, dc = width // NX, NX * rows, 2 * wr
    tokens, columns = NZ * shard, NX * dc
    factor = 1.0 / math.sqrt(inputs.shape[0] * lax.axis_size("gx"))
    vmem, anywhere = pl.BlockSpec(memory_space=pltpu.VMEM), pl.BlockSpec(memory_space=pl.ANY)
    dma = pltpu.SemaphoreType.DMA
    return pl.pallas_call(
        functools.partial(kernel, factor),
        out_shape=(
            jax.ShapeDtypeStruct(inputs.shape, BF16),
            jax.ShapeDtypeStruct(gate_weight.shape, BF16),
            jax.ShapeDtypeStruct(up_weight.shape, BF16),
        ),
        in_specs=[vmem, vmem, vmem, vmem, anywhere, anywhere],
        out_specs=(vmem, anywhere, anywhere),
        scratch_shapes=[
            pltpu.VMEM((NX, 2, rows, fq), BF16),
            pltpu.VMEM((2, NZ, shard, fq), BF16),
            pltpu.VMEM((2, columns, fq), BF16),
            pltpu.VMEM((dc, NZH * shard), BF16),
            pltpu.VMEM((columns, tokens), BF16),
            pltpu.VMEM((NZ, shard, columns), BF16),
            pltpu.VMEM((NY, NZH, shard, columns), BF16),
            pltpu.VMEM((NX, NZH, shard, dc), BF16),
            pltpu.VMEM((NX, NZH, shard, dc), BF16),
            pltpu.VMEM((2, NX, dc, fq), F32),
            pltpu.VMEM((2, NX, wr, fq), BF16),
            pltpu.VMEM((2, NX, wr, fq), BF16),
            pltpu.VMEM((2, NX, wr, fq), BF16),
            dma((NX,)), dma((NX,)),
            dma((2, 2, NZ // 2, 2)), dma((2, 2, NZ // 2, 2)),
            dma((2, NX)), dma((2, NX)),
            dma((2, NX)), dma((2, NX)),
            dma((NX,)), dma((NX,)),
            dma((NY,)), dma((NY,)),
            dma((NZ,)), dma((NY, NZH)),
            dma((NX,)), dma((NX,)),
            dma((2, NX)), dma((2, NX)),
            dma((2, NX)), dma((2, NX)),
        ],
        compiler_params=pltpu.CompilerParams(
            collective_id=0, has_side_effects=True, vmem_limit_bytes=56 << 20
        ),
        cost_estimate=pl.CostEstimate(
            flops=8 * tokens * columns * fq, bytes_accessed=12 * wr * width, transcendentals=rows * width
        ),
        name="swiglu_backward",
    )(inputs, hidden_grad, gate_pre, up_pre, gate_weight, up_weight)


def solution(mesh):
    placed = (
        P("gx", ("gy", "gz")),
        P(("gx", "gy"), "gz"),
        P(("gx", "gy"), "gz"),
        P(("gx", "gy"), "gz"),
        P(("gy", "gx"), "gz"),
        P(("gy", "gx"), "gz"),
    )
    return jax.shard_map(
        body,
        mesh=mesh,
        in_specs=placed,
        out_specs=(P("gx", ("gy", "gz")), P(("gy", "gx"), "gz"), P(("gy", "gx"), "gz")),
        check_vma=False,
    )
```

```python
import functools
import math

import jax
import jax.numpy as jnp
from jax import lax
from jax.experimental import pallas as pl
from jax.experimental.pallas import tpu as pltpu
from jax.sharding import PartitionSpec as P

MESH = pl.DeviceIdType.MESH
BF16, F32 = jnp.bfloat16, jnp.float32

NX, NY, NZH, NZL = 4, 4, 2, 4
NZ = NZH * NZL


def aligned(index, step, size):
    return pl.ds(pl.multiple_of(index * step, step), size)


def kernel(
    factor,
    x_ref, h_ref, g_ref, u_ref, wg_ref, wu_ref,
    dx_ref, dwg_ref, dwu_ref,
    g0, gbuf, wbuf, xt0, xbuf, dxs, dxr, dxp, dxq, dxo, dwt, dws, dwr, dwf,
    ga_s, ga_r, gr_s, gr_r, wa_s, wa_r, wc_s, wc_r, xa_s, xa_r, xb_s, xb_r, xc_s, xc_r,
    dy_s, dy_r, dq_s, dq_r, do_s, do_r, ec_s, ec_r, eo_s, eo_r,
):
    gx, gy, gz = lax.axis_index("gx"), lax.axis_index("gy"), lax.axis_index("gz")
    x, zh, y, zl, c = gy // NZH, gy % NZH, gz, gx // 2, gx % 2
    z = zh * NZL + zl
    rows = h_ref.shape[0]
    fq = h_ref.shape[1] // NX
    wr = wg_ref.shape[0]
    dc = 2 * wr
    shard = NX * rows
    blk = NZH * shard
    half = shard // 2
    w_refs, dw_refs = (wg_ref, wu_ref), (dwg_ref, dwu_ref)

    def dev(xx, yy, zz, cc):
        return ((zz % NZL) * 2 + cc, xx * NZH + zz // NZL, yy)

    def remote(src, dst, ss, rs, to):
        return pltpu.make_async_remote_copy(
            src_ref=src, dst_ref=dst, send_sem=ss, recv_sem=rs, device_id=to, device_id_type=MESH
        )

    here = dev(x, y, z, c)
    pair = dev(x, y, z, 1 - c)
    xs = [(x + k) % NX for k in range(NX)]
    ys = [(y + k) % NY for k in range(NY)]
    up, down = dev(x, y, (z + 1) % NZ, c), dev(x, y, (z + NZ - 1) % NZ, c)
    swapped = dev(x, zl, zh * NZL + y, c)
    on_diag = y == zl

    def landed(ref, sem):
        remote(ref, ref, sem, sem, pair).wait_recv()

    def sent(ref, sem):
        remote(ref, ref, sem, sem, pair).wait_send()

    barrier = pltpu.get_barrier_semaphore()

    def greet(to):
        pl.semaphore_signal(barrier, inc=1, device_id=to, device_id_type=MESH)

    for k in range(1, NX):
        greet(dev(xs[k], y, z, c))
    for k in range(1, NY):
        greet(dev(x, ys[k], z, c))
    greet(up)
    greet(down)
    greet(pair)

    @pl.when(on_diag)
    def _():
        pl.semaphore_wait(barrier, (NX - 1) + (NY - 1) + 3)

    @pl.when(jnp.logical_not(on_diag))
    def _():
        greet(swapped)
        pl.semaphore_wait(barrier, (NX - 1) + (NY - 1) + 4)

    for q in range(NX):
        part = slice(q * fq, (q + 1) * fq)
        hh = h_ref[:, part].astype(F32)
        gg = g_ref[:, part].astype(F32)
        uu = u_ref[:, part].astype(F32)
        sq = jax.nn.sigmoid(gg)
        g0[q, 0] = (hh * uu * sq * (1.0 + gg * (1.0 - sq))).astype(BF16)
        g0[q, 1] = (hh * gg * sq).astype(BF16)

    def place(zz):
        zz = zz % NZ
        return (zz % NZL) * NZH + zz // NZL

    mine = place(z)
    g_mine = gbuf.at[:, mine, aligned(x, rows, rows), :]
    pltpu.make_async_copy(g0.at[x], g_mine, ga_r.at[x]).start()
    for k in range(1, NX):
        remote(g0.at[xs[k]], g_mine, ga_s.at[k], ga_r.at[x], dev(xs[k], y, z, c)).start()

    xin = x_ref[...].astype(F32)
    xp = jnp.concatenate(
        [xin[(i * NZH + j) * rows:(i * NZH + j + 1) * rows] for j in range(NZH) for i in range(NX)], axis=0
    )
    xt0[...] = xp.T.astype(BF16)
    x_dst = xbuf.at[aligned(x, dc, dc), aligned(zl, blk, blk)]

    @pl.when(on_diag)
    def _():
        pltpu.make_async_copy(xt0, x_dst, xa_r).start()

    @pl.when(jnp.logical_not(on_diag))
    def _():
        remote(xt0, x_dst, xa_s, xa_r, swapped).start()

    def w_src(gu, q):
        return w_refs[gu].at[:, aligned(q, fq, fq)]

    def w_rows(gu, i, cc):
        return wbuf.at[gu, aligned(i * 2 + cc, wr, wr), :]

    def w_send(gu, k):
        return remote(w_src(gu, xs[k]), w_rows(gu, x, c), wa_s.at[gu, k], wa_r.at[gu, x], dev(xs[k], y, z, c))

    def w_start(gu):
        pltpu.make_async_copy(w_src(gu, x), w_rows(gu, x, c), wa_r.at[gu, x]).start()
        for k in range(1, NX):
            w_send(gu, k).start()

    def w_forward(gu):
        for i in range(NX):
            landed(w_rows(gu, i, c), wa_r.at[gu, i])
            remote(w_rows(gu, i, c), w_rows(gu, i, c), wc_s.at[gu, i], wc_r.at[gu, i], pair).start()

    def ring_ref(gu, zz, part):
        return gbuf.at[gu, place(zz), pl.ds(part * half, half), :]

    def ring_send(gu, d, s, part):
        ref = ring_ref(gu, z + (NZ - s if d == 0 else s), part)
        return remote(ref, ref, gr_s.at[gu, d, s, part], gr_r.at[gu, d, s, part], up if d == 0 else down)

    def ring_landed(gu, d, s, part):
        landed(ring_ref(gu, z + (NZ - 1 - s if d == 0 else 1 + s), part), gr_r.at[gu, d, s, part])

    def part_of(d, j):
        return j if d == 0 else 1 - j

    last = NZ // 2 - 1

    def ring_first(gu):
        for j in range(2):
            for d in range(2):
                ring_send(gu, d, 0, part_of(d, j)).start()

    def ring_step(gu, s, j):
        for d in range(2):
            ring_landed(gu, d, s - 1, part_of(d, j))
            ring_send(gu, d, s, part_of(d, j)).start()

    def ring_end(gu):
        for d in range(2):
            ring_landed(gu, d, last - 1, part_of(d, 1))
        for d in range(2):
            ring_landed(gu, d, last, part_of(d, 0))

    def x_piece(i, k):
        return xbuf.at[aligned(i, dc, dc), aligned(k, blk, blk)]

    def x_along_y(i):
        for k in range(1, NY):
            remote(x_piece(i, y), x_piece(i, y), xb_s.at[i, k], xb_r.at[i, y], dev(x, ys[k], z, c)).start()

    def x_start():
        landed(x_piece(x, y), xa_r)
        for k in range(1, NX):
            remote(x_piece(x, y), x_piece(x, y), xc_s.at[k], xc_r.at[x], dev(xs[k], y, z, c)).start()
        x_along_y(x)

    def x_forward():
        for k in range(1, NX):
            landed(x_piece(xs[k], y), xc_r.at[xs[k]])
            x_along_y(xs[k])

    def x_end():
        for i in range(NX):
            for k in range(1, NY):
                landed(x_piece(i, ys[k]), xb_r.at[i, ys[k]])

    def dw_out(gu, q):
        return dw_refs[gu].at[:, aligned(q, fq, fq)]

    def dw_send(gu, k):
        return remote(dwf.at[gu, xs[k]], dw_out(gu, x), eo_s.at[gu, k], eo_r.at[gu, x], dev(xs[k], y, z, c))

    def dw_pair(gu, i):
        return remote(dws.at[gu, i], dwr.at[gu, i], ec_s.at[gu, i], ec_r.at[gu, i], pair)

    def dw_compute(gu):
        tokens = gbuf.at[gu]

        @pl.loop(0, NX)
        def _(i):
            lhs = xbuf[aligned(i, dc, dc), :]
            rhs = tokens[...].reshape(NZ * shard, fq)
            dwt[gu, i] = jnp.dot(lhs, rhs, preferred_element_type=F32)
            dws[gu, i] = dwt[gu, i, aligned(1 - c, wr, wr), :].astype(BF16)
            dw_pair(gu, i).start()

    def dw_finish(gu):
        for k in range(NX - 1, -1, -1):
            i = xs[k]
            landed(dwr.at[gu, i], ec_r.at[gu, i])
            total = dwt[gu, i, aligned(c, wr, wr), :] + dwr[gu, i].astype(F32)
            dwf[gu, i] = (total * factor).astype(BF16)
            if k:
                dw_send(gu, k).start()
            else:
                pltpu.make_async_copy(dwf.at[gu, i], dw_out(gu, x), eo_r.at[gu, x]).start()

    def dx_parts(p, d_zh, d_zl):
        return dxs.at[p], dxr.at[y, d_zh]

    def dx_shard(zz):
        zz = zz % NZ
        p, j, owner = place(zz), zz // NZL, zz % NZL

        @pl.loop(0, NX)
        def _(i):
            columns = aligned(i, dc, dc)
            total = lax.dot_general(
                gbuf[0, p], wbuf[0, columns, :], (((1,), (1,)), ((), ())), preferred_element_type=F32
            ) + lax.dot_general(
                gbuf[1, p], wbuf[1, columns, :], (((1,), (1,)), ((), ())), preferred_element_type=F32
            )
            dxs[p, :, columns] = total.astype(BF16)

        @pl.when(owner == y)
        def _():
            pltpu.make_async_copy(dxs.at[p], dxr.at[y, j], dy_r.at[y, j]).start()

        @pl.when(owner != y)
        def _():
            remote(dxs.at[p], dxr.at[y, j], dy_s.at[p], dy_r.at[y, j], dev(x, owner, z, c)).start()

    def w_end():
        for gu in range(2):
            for i in range(NX):
                landed(w_rows(gu, i, 1 - c), wc_r.at[gu, i])

    for i in range(NX):
        landed(gbuf.at[:, mine, pl.ds(i * rows, rows), :], ga_r.at[i])
    ring_first(0)
    w_start(0)
    x_start()
    ring_step(0, 1, 0)
    ring_step(0, 1, 1)
    x_forward()
    w_start(1)
    ring_step(0, 2, 0)
    w_forward(0)
    ring_step(0, 2, 1)
    ring_step(0, 3, 0)
    ring_first(1)
    ring_end(0)
    ring_step(1, 1, 0)
    ring_step(1, 1, 1)
    w_forward(1)
    x_end()
    dw_compute(0)
    ring_step(1, 2, 0)
    w_end()
    dx_shard(z)
    dw_finish(0)
    ring_step(1, 2, 1)
    dx_shard(z + NZ - 1)
    dx_shard(z + 1)
    ring_step(1, 3, 0)
    dx_shard(z + NZ - 2)
    dx_shard(z + 2)
    ring_end(1)
    dx_shard(z + NZ - 3)
    dx_shard(z + 3)
    dx_shard(z + 4)
    dw_compute(1)
    dw_finish(1)

    for i in range(NY):
        for j in range(NZH):
            landed(dxr.at[i, j], dy_r.at[i, j])
    for i in range(NX):
        columns = slice(i * dc, (i + 1) * dc)
        total = dxr[0, :, :, columns].astype(F32)
        for k in range(1, NY):
            total = total + dxr[k, :, :, columns].astype(F32)
        dxp[i] = total.astype(BF16)

    pltpu.make_async_copy(dxp.at[x], dxq.at[x], dq_r.at[x]).start()
    for k in range(1, NX):
        remote(dxp.at[xs[k]], dxq.at[x], dq_s.at[k], dq_r.at[x], dev(xs[k], y, z, c)).start()
    for i in range(NX):
        landed(dxq.at[i], dq_r.at[i])
    for j in range(NZH):
        for i in range(NX):
            part = slice(i * rows, (i + 1) * rows)
            total = dxq[0, j, part, :].astype(F32)
            for k in range(1, NX):
                total = total + dxq[k, j, part, :].astype(F32)
            dxo[(i * NZH + j) * rows:(i * NZH + j + 1) * rows, :] = total.astype(BF16)

    @pl.when(on_diag)
    def _():
        pltpu.make_async_copy(dxo, dx_ref, do_r).start()

    @pl.when(jnp.logical_not(on_diag))
    def _():
        remote(dxo, dx_ref, do_s, do_r, swapped).start()

    landed(dx_ref, do_r)

    for gu in range(2):
        for i in range(NX):
            landed(dw_out(gu, i), eo_r.at[gu, i])
    for k in range(1, NX):
        sent(g0.at[xs[k]], ga_s.at[k])
        sent(x_piece(x, y), xc_s.at[k])
        for i in range(NX):
            sent(x_piece(i, y), xb_s.at[i, k])
        sent(dxp.at[xs[k]], dq_s.at[k])
        for gu in range(2):
            sent(w_src(gu, xs[k]), wa_s.at[gu, k])
            sent(dwf.at[gu, xs[k]], eo_s.at[gu, k])

    @pl.when(jnp.logical_not(on_diag))
    def _():
        sent(xt0, xa_s)
        sent(dxo, do_s)

    for gu in range(2):
        for i in range(NX):
            sent(w_rows(gu, i, c), wc_s.at[gu, i])
            sent(dws.at[gu, i], ec_s.at[gu, i])
        for s in range(last + 1):
            for j in range(2 if s < last else 1):
                for d in range(2):
                    ring_send(gu, d, s, part_of(d, j)).wait_send()
    for p in range(NZ):

        @pl.when(p // NZH != y)
        def _():
            sent(dxs.at[p], dy_s.at[p])


def body(inputs, hidden_grad, gate_pre, up_pre, gate_weight, up_weight):
    rows, width = hidden_grad.shape
    wr = gate_weight.shape[0]
    fq, shard, dc = width // NX, NX * rows, 2 * wr
    tokens, columns = NZ * shard, NX * dc
    factor = 1.0 / math.sqrt(inputs.shape[0] * lax.axis_size("gx"))
    vmem, anywhere = pl.BlockSpec(memory_space=pltpu.VMEM), pl.BlockSpec(memory_space=pl.ANY)
    dma = pltpu.SemaphoreType.DMA
    return pl.pallas_call(
        functools.partial(kernel, factor),
        out_shape=(
            jax.ShapeDtypeStruct(inputs.shape, BF16),
            jax.ShapeDtypeStruct(gate_weight.shape, BF16),
            jax.ShapeDtypeStruct(up_weight.shape, BF16),
        ),
        in_specs=[vmem, vmem, vmem, vmem, anywhere, anywhere],
        out_specs=(vmem, anywhere, anywhere),
        scratch_shapes=[
            pltpu.VMEM((NX, 2, rows, fq), BF16),
            pltpu.VMEM((2, NZ, shard, fq), BF16),
            pltpu.VMEM((2, columns, fq), BF16),
            pltpu.VMEM((dc, NZH * shard), BF16),
            pltpu.VMEM((columns, tokens), BF16),
            pltpu.VMEM((NZ, shard, columns), BF16),
            pltpu.VMEM((NY, NZH, shard, columns), BF16),
            pltpu.VMEM((NX, NZH, shard, dc), BF16),
            pltpu.VMEM((NX, NZH, shard, dc), BF16),
            pltpu.VMEM((NZH * shard, dc), BF16),
            pltpu.VMEM((2, NX, dc, fq), F32),
            pltpu.VMEM((2, NX, wr, fq), BF16),
            pltpu.VMEM((2, NX, wr, fq), BF16),
            pltpu.VMEM((2, NX, wr, fq), BF16),
            dma((NX,)), dma((NX,)),
            dma((2, 2, NZ // 2, 2)), dma((2, 2, NZ // 2, 2)),
            dma((2, NX)), dma((2, NX)),
            dma((2, NX)), dma((2, NX)),
            dma, dma,
            dma((NX, NY)), dma((NX, NY)),
            dma((NX,)), dma((NX,)),
            dma((NZ,)), dma((NY, NZH)),
            dma((NX,)), dma((NX,)),
            dma, dma,
            dma((2, NX)), dma((2, NX)),
            dma((2, NX)), dma((2, NX)),
        ],
        compiler_params=pltpu.CompilerParams(
            collective_id=0, has_side_effects=True, vmem_limit_bytes=56 << 20
        ),
        cost_estimate=pl.CostEstimate(
            flops=8 * tokens * columns * fq, bytes_accessed=12 * wr * width, transcendentals=rows * width
        ),
        name="swiglu_backward",
    )(inputs, hidden_grad, gate_pre, up_pre, gate_weight, up_weight)


def solution(mesh):
    placed = (
        P("gx", ("gy", "gz")),
        P(("gx", "gy"), "gz"),
        P(("gx", "gy"), "gz"),
        P(("gx", "gy"), "gz"),
        P(("gy", "gx"), "gz"),
        P(("gy", "gx"), "gz"),
    )
    return jax.shard_map(
        body,
        mesh=mesh,
        in_specs=placed,
        out_specs=(P("gx", ("gy", "gz")), P(("gy", "gx"), "gz"), P(("gy", "gx"), "gz")),
        check_vma=False,
    )
```

```python
import functools
import math

import jax
import jax.numpy as jnp
from jax import lax
from jax.experimental import pallas as pl
from jax.experimental.pallas import tpu as pltpu
from jax.sharding import PartitionSpec as P

MESH = pl.DeviceIdType.MESH
BF16, F32 = jnp.bfloat16, jnp.float32

NX, NY, NZH, NZL = 4, 4, 2, 4
NZ = NZH * NZL


def aligned(index, step, size):
    return pl.ds(pl.multiple_of(index * step, step), size)


def kernel(
    factor,
    x_ref, h_ref, g_ref, u_ref, wg_ref, wu_ref,
    dx_ref, dwg_ref, dwu_ref,
    g0, gbuf, wbuf, xt0, xbuf, dxs, dxr, dxp, dxq, dxo, dwt, dws, dwr, dwf,
    ga_s, ga_r, gr_s, gr_r, wa_s, wa_r, wc_s, wc_r, xa_s, xa_r, xb_s, xb_r, xc_s, xc_r,
    dy_s, dy_r, dq_s, dq_r, do_s, do_r, ec_s, ec_r, eo_s, eo_r,
):
    gx, gy, gz = lax.axis_index("gx"), lax.axis_index("gy"), lax.axis_index("gz")
    x, zh, y, zl, c = gy // NZH, gy % NZH, gz, gx // 2, gx % 2
    z = zh * NZL + zl
    rows = h_ref.shape[0]
    fq = h_ref.shape[1] // NX
    wr = wg_ref.shape[0]
    dc = 2 * wr
    shard = NX * rows
    blk = NZH * shard
    half = shard // 2
    w_refs, dw_refs = (wg_ref, wu_ref), (dwg_ref, dwu_ref)

    def dev(xx, yy, zz, cc):
        return ((zz % NZL) * 2 + cc, xx * NZH + zz // NZL, yy)

    def remote(src, dst, ss, rs, to):
        return pltpu.make_async_remote_copy(
            src_ref=src, dst_ref=dst, send_sem=ss, recv_sem=rs, device_id=to, device_id_type=MESH
        )

    here = dev(x, y, z, c)
    pair = dev(x, y, z, 1 - c)
    xs = [(x + k) % NX for k in range(NX)]
    ys = [(y + k) % NY for k in range(NY)]
    up, down = dev(x, y, (z + 1) % NZ, c), dev(x, y, (z + NZ - 1) % NZ, c)
    swapped = dev(x, zl, zh * NZL + y, c)
    on_diag = y == zl

    def landed(ref, sem):
        remote(ref, ref, sem, sem, pair).wait_recv()

    def sent(ref, sem):
        remote(ref, ref, sem, sem, pair).wait_send()

    barrier = pltpu.get_barrier_semaphore()

    def greet(to):
        pl.semaphore_signal(barrier, inc=1, device_id=to, device_id_type=MESH)

    for k in range(1, NX):
        greet(dev(xs[k], y, z, c))
    for k in range(1, NY):
        greet(dev(x, ys[k], z, c))
    greet(up)
    greet(down)
    greet(pair)

    for k in range(NY):

        @pl.when(jnp.logical_or(y != zl, y != k))
        def _():
            greet(dev(x, k, zh * NZL + y, c))

    greetings = (NX - 1) + (NY - 1) + 3 + NZL

    @pl.when(on_diag)
    def _():
        pl.semaphore_wait(barrier, greetings - 1)

    @pl.when(jnp.logical_not(on_diag))
    def _():
        pl.semaphore_wait(barrier, greetings)

    for q in range(NX):
        part = slice(q * fq, (q + 1) * fq)
        hh = h_ref[:, part].astype(F32)
        gg = g_ref[:, part].astype(F32)
        uu = u_ref[:, part].astype(F32)
        sq = jax.nn.sigmoid(gg)
        g0[q, 0] = (hh * uu * sq * (1.0 + gg * (1.0 - sq))).astype(BF16)
        g0[q, 1] = (hh * gg * sq).astype(BF16)

    def place(zz):
        zz = zz % NZ
        return (zz % NZL) * NZH + zz // NZL

    mine = place(z)
    g_mine = gbuf.at[:, mine, aligned(x, rows, rows), :]
    pltpu.make_async_copy(g0.at[x], g_mine, ga_r.at[x]).start()
    for k in range(1, NX):
        remote(g0.at[xs[k]], g_mine, ga_s.at[k], ga_r.at[x], dev(xs[k], y, z, c)).start()

    xin = x_ref[...].astype(F32)
    xp = jnp.concatenate(
        [xin[(i * NZH + j) * rows:(i * NZH + j + 1) * rows] for j in range(NZH) for i in range(NX)], axis=0
    )
    xt0[...] = xp.T.astype(BF16)
    x_dst = xbuf.at[aligned(x, dc, dc), aligned(zl, blk, blk)]

    @pl.when(on_diag)
    def _():
        pltpu.make_async_copy(xt0, x_dst, xa_r).start()

    @pl.when(jnp.logical_not(on_diag))
    def _():
        remote(xt0, x_dst, xa_s, xa_r, swapped).start()

    def w_src(gu, q):
        return w_refs[gu].at[:, aligned(q, fq, fq)]

    def w_rows(gu, i, cc):
        return wbuf.at[gu, aligned(i * 2 + cc, wr, wr), :]

    def w_send(gu, k):
        return remote(w_src(gu, xs[k]), w_rows(gu, x, c), wa_s.at[gu, k], wa_r.at[gu, x], dev(xs[k], y, z, c))

    def w_start(gu):
        pltpu.make_async_copy(w_src(gu, x), w_rows(gu, x, c), wa_r.at[gu, x]).start()
        for k in range(1, NX):
            w_send(gu, k).start()

    def w_forward(gu):
        for i in range(NX):
            landed(w_rows(gu, i, c), wa_r.at[gu, i])
            remote(w_rows(gu, i, c), w_rows(gu, i, c), wc_s.at[gu, i], wc_r.at[gu, i], pair).start()

    def ring_ref(gu, zz, part):
        return gbuf.at[gu, place(zz), pl.ds(part * half, half), :]

    def ring_send(gu, d, s, part):
        ref = ring_ref(gu, z + (NZ - s if d == 0 else s), part)
        return remote(ref, ref, gr_s.at[gu, d, s, part], gr_r.at[gu, d, s, part], up if d == 0 else down)

    def ring_landed(gu, d, s, part):
        landed(ring_ref(gu, z + (NZ - 1 - s if d == 0 else 1 + s), part), gr_r.at[gu, d, s, part])

    def part_of(d, j):
        return j if d == 0 else 1 - j

    last = NZ // 2 - 1

    def ring_first(gu):
        for j in range(2):
            for d in range(2):
                ring_send(gu, d, 0, part_of(d, j)).start()

    def ring_step(gu, s, j):
        for d in range(2):
            ring_landed(gu, d, s - 1, part_of(d, j))
            ring_send(gu, d, s, part_of(d, j)).start()

    def ring_near_end(gu):
        for d in range(2):
            ring_landed(gu, d, last - 1, part_of(d, 1))

    def ring_end(gu):
        for d in range(2):
            ring_landed(gu, d, last, part_of(d, 0))

    def x_piece(i, k):
        return xbuf.at[aligned(i, dc, dc), aligned(k, blk, blk)]

    def x_along_y(i):
        for k in range(1, NY):
            remote(x_piece(i, y), x_piece(i, y), xb_s.at[i, k], xb_r.at[i, y], dev(x, ys[k], z, c)).start()

    def x_start():
        landed(x_piece(x, y), xa_r)
        for k in range(1, NX):
            remote(x_piece(x, y), x_piece(x, y), xc_s.at[k], xc_r.at[x], dev(xs[k], y, z, c)).start()
        x_along_y(x)

    def x_forward():
        for k in range(1, NX):
            landed(x_piece(xs[k], y), xc_r.at[xs[k]])
            x_along_y(xs[k])

    def x_end():
        for i in range(NX):
            for k in range(1, NY):
                landed(x_piece(i, ys[k]), xb_r.at[i, ys[k]])

    def dw_out(gu, q):
        return dw_refs[gu].at[:, aligned(q, fq, fq)]

    def dw_send(gu, k):
        return remote(dwf.at[gu, xs[k]], dw_out(gu, x), eo_s.at[gu, k], eo_r.at[gu, x], dev(xs[k], y, z, c))

    def dw_pair(gu, i):
        return remote(dws.at[gu, i], dwr.at[gu, i], ec_s.at[gu, i], ec_r.at[gu, i], pair)

    def dw_compute(gu, first=0, end=NX):
        tokens = gbuf.at[gu]

        @pl.loop(first, end)
        def _(i):
            lhs = xbuf[aligned(i, dc, dc), :]
            rhs = tokens[...].reshape(NZ * shard, fq)
            dwt[gu, i] = jnp.dot(lhs, rhs, preferred_element_type=F32)
            dws[gu, i] = dwt[gu, i, aligned(1 - c, wr, wr), :].astype(BF16)
            dw_pair(gu, i).start()

    def dw_finish(gu):
        for k in range(NX - 1, -1, -1):
            i = xs[k]
            landed(dwr.at[gu, i], ec_r.at[gu, i])
            total = dwt[gu, i, aligned(c, wr, wr), :] + dwr[gu, i].astype(F32)
            dwf[gu, i] = (total * factor).astype(BF16)
            if k:
                dw_send(gu, k).start()
            else:
                pltpu.make_async_copy(dwf.at[gu, i], dw_out(gu, x), eo_r.at[gu, x]).start()

    def dx_rows(p, k):
        return dxs.at[p, aligned(k, rows, rows), :]

    def dx_shard(zz):
        zz = zz % NZ
        p = place(zz)

        @pl.loop(0, NX)
        def _(i):
            columns = aligned(i, dc, dc)
            total = lax.dot_general(
                gbuf[0, p], wbuf[0, columns, :], (((1,), (1,)), ((), ())), preferred_element_type=F32
            ) + lax.dot_general(
                gbuf[1, p], wbuf[1, columns, :], (((1,), (1,)), ((), ())), preferred_element_type=F32
            )
            dxs[p, :, columns] = total.astype(BF16)

        pltpu.make_async_copy(dx_rows(p, y), dxr.at[y, p], dy_r.at[p, y]).start()
        for k in range(1, NY):
            remote(dx_rows(p, ys[k]), dxr.at[y, p], dy_s.at[p, k], dy_r.at[p, y], dev(x, ys[k], z, c)).start()

    def w_end():
        for gu in range(2):
            for i in range(NX):
                landed(w_rows(gu, i, 1 - c), wc_r.at[gu, i])

    def dx_sum(*shards):
        for zz in shards:
            p = place(zz)
            for i in range(NY):
                landed(dxr.at[i, p], dy_r.at[p, i])
            total = dxr[0, p].astype(F32)
            for k in range(1, NY):
                total = total + dxr[k, p].astype(F32)
            for i in range(NX):
                dxp[i, p] = total[:, i * dc:(i + 1) * dc].astype(BF16)
            pltpu.make_async_copy(dxp.at[x, p], dxq.at[x, p], dq_r.at[p, x]).start()
            for k in range(1, NX):
                remote(dxp.at[xs[k], p], dxq.at[x, p], dq_s.at[p, k], dq_r.at[p, x], dev(xs[k], y, z, c)).start()

    def dx_out(*shards):
        for zz in shards:
            zz = zz % NZ
            p, j, owner = place(zz), zz // NZL, zz % NZL
            for i in range(NX):
                landed(dxq.at[i, p], dq_r.at[p, i])
            total = dxq[0, p].astype(F32)
            for k in range(1, NX):
                total = total + dxq[k, p].astype(F32)
            dxo[p] = total.astype(BF16)
            target = dx_ref.at[aligned(y * NZH + j, rows, rows), :]
            stays = jnp.logical_and(on_diag, owner == zl)

            @pl.when(stays)
            def _():
                pltpu.make_async_copy(dxo.at[p], target, do_r.at[y, j]).start()

            @pl.when(jnp.logical_not(stays))
            def _():
                remote(dxo.at[p], target, do_s.at[p], do_r.at[y, j], dev(x, zl, zh * NZL + owner, c)).start()

    def dx_end():
        for i in range(NY):
            for j in range(NZH):
                landed(dx_ref.at[pl.ds((i * NZH + j) * rows, rows), :], do_r.at[i, j])

    for i in range(NX):
        landed(gbuf.at[:, mine, pl.ds(i * rows, rows), :], ga_r.at[i])
    ring_first(0)
    w_start(0)
    x_start()
    ring_step(0, 1, 0)
    ring_step(0, 1, 1)
    x_forward()
    w_start(1)
    ring_step(0, 2, 0)
    w_forward(0)
    ring_step(0, 2, 1)
    ring_step(0, 3, 0)
    ring_first(1)
    ring_near_end(0)
    ring_end(0)
    ring_step(1, 1, 0)
    ring_step(1, 1, 1)
    w_forward(1)
    x_end()
    dw_compute(0)
    ring_step(1, 2, 0)
    w_end()
    dx_shard(z)
    dw_finish(0)
    ring_step(1, 2, 1)
    dx_shard(z + NZ - 1)
    dx_shard(z + 1)
    ring_step(1, 3, 0)
    dx_shard(z + NZ - 2)
    dx_shard(z + 2)
    ring_near_end(1)
    dx_shard(z + NZ - 3)
    dx_shard(z + 3)
    dx_sum(z, z + NZ - 1, z + 1, z + NZ - 2, z + 2)
    ring_end(1)
    dx_shard(z + 4)
    dw_compute(1)
    dx_sum(z + NZ - 3, z + 3, z + 4)
    dx_out(z, z + NZ - 1, z + 1, z + NZ - 2, z + 2)
    dw_finish(1)
    dx_out(z + NZ - 3, z + 3, z + 4)
    dx_end()

    for gu in range(2):
        for i in range(NX):
            landed(dw_out(gu, i), eo_r.at[gu, i])
    for k in range(1, NX):
        sent(g0.at[xs[k]], ga_s.at[k])
        sent(x_piece(x, y), xc_s.at[k])
        for i in range(NX):
            sent(x_piece(i, y), xb_s.at[i, k])
        for p in range(NZ):
            sent(dx_rows(p, ys[k]), dy_s.at[p, k])
            sent(dxp.at[xs[k], p], dq_s.at[p, k])
        for gu in range(2):
            sent(w_src(gu, xs[k]), wa_s.at[gu, k])
            sent(dwf.at[gu, xs[k]], eo_s.at[gu, k])

    @pl.when(jnp.logical_not(on_diag))
    def _():
        sent(xt0, xa_s)

    for gu in range(2):
        for i in range(NX):
            sent(w_rows(gu, i, c), wc_s.at[gu, i])
            sent(dws.at[gu, i], ec_s.at[gu, i])
        for s in range(last + 1):
            for j in range(2 if s < last else 1):
                for d in range(2):
                    ring_send(gu, d, s, part_of(d, j)).wait_send()
    for p in range(NZ):

        @pl.when(jnp.logical_not(jnp.logical_and(on_diag, p // NZH == zl)))
        def _():
            sent(dxo.at[p], do_s.at[p])


def body(inputs, hidden_grad, gate_pre, up_pre, gate_weight, up_weight):
    rows, width = hidden_grad.shape
    wr = gate_weight.shape[0]
    fq, shard, dc = width // NX, NX * rows, 2 * wr
    tokens, columns = NZ * shard, NX * dc
    factor = 1.0 / math.sqrt(inputs.shape[0] * lax.axis_size("gx"))
    vmem, anywhere = pl.BlockSpec(memory_space=pltpu.VMEM), pl.BlockSpec(memory_space=pl.ANY)
    dma = pltpu.SemaphoreType.DMA
    return pl.pallas_call(
        functools.partial(kernel, factor),
        out_shape=(
            jax.ShapeDtypeStruct(inputs.shape, BF16),
            jax.ShapeDtypeStruct(gate_weight.shape, BF16),
            jax.ShapeDtypeStruct(up_weight.shape, BF16),
        ),
        in_specs=[vmem, vmem, vmem, vmem, anywhere, anywhere],
        out_specs=(vmem, anywhere, anywhere),
        scratch_shapes=[
            pltpu.VMEM((NX, 2, rows, fq), BF16),
            pltpu.VMEM((2, NZ, shard, fq), BF16),
            pltpu.VMEM((2, columns, fq), BF16),
            pltpu.VMEM((dc, NZH * shard), BF16),
            pltpu.VMEM((columns, tokens), BF16),
            pltpu.VMEM((NZ, shard, columns), BF16),
            pltpu.VMEM((NY, NZ, rows, columns), BF16),
            pltpu.VMEM((NX, NZ, rows, dc), BF16),
            pltpu.VMEM((NX, NZ, rows, dc), BF16),
            pltpu.VMEM((NZ, rows, dc), BF16),
            pltpu.VMEM((2, NX, dc, fq), F32),
            pltpu.VMEM((2, NX, wr, fq), BF16),
            pltpu.VMEM((2, NX, wr, fq), BF16),
            pltpu.VMEM((2, NX, wr, fq), BF16),
            dma((NX,)), dma((NX,)),
            dma((2, 2, NZ // 2, 2)), dma((2, 2, NZ // 2, 2)),
            dma((2, NX)), dma((2, NX)),
            dma((2, NX)), dma((2, NX)),
            dma, dma,
            dma((NX, NY)), dma((NX, NY)),
            dma((NX,)), dma((NX,)),
            dma((NZ, NY)), dma((NZ, NY)),
            dma((NZ, NX)), dma((NZ, NX)),
            dma((NZ,)), dma((NY, NZH)),
            dma((2, NX)), dma((2, NX)),
            dma((2, NX)), dma((2, NX)),
        ],
        compiler_params=pltpu.CompilerParams(
            collective_id=0, has_side_effects=True, vmem_limit_bytes=56 << 20
        ),
        cost_estimate=pl.CostEstimate(
            flops=8 * tokens * columns * fq, bytes_accessed=12 * wr * width, transcendentals=rows * width
        ),
        name="swiglu_backward",
    )(inputs, hidden_grad, gate_pre, up_pre, gate_weight, up_weight)


def solution(mesh):
    placed = (
        P("gx", ("gy", "gz")),
        P(("gx", "gy"), "gz"),
        P(("gx", "gy"), "gz"),
        P(("gx", "gy"), "gz"),
        P(("gy", "gx"), "gz"),
        P(("gy", "gx"), "gz"),
    )
    return jax.shard_map(
        body,
        mesh=mesh,
        in_specs=placed,
        out_specs=(P("gx", ("gy", "gz")), P(("gy", "gx"), "gz"), P(("gy", "gx"), "gz")),
        check_vma=False,
    )
```

```python
import functools
import math

import jax
import jax.numpy as jnp
from jax import lax
from jax.experimental import pallas as pl
from jax.experimental.pallas import tpu as pltpu
from jax.sharding import PartitionSpec as P

MESH = pl.DeviceIdType.MESH
BF16, F32 = jnp.bfloat16, jnp.float32

NX, NY, NZH, NZL = 4, 4, 2, 4
NZ = NZH * NZL


def aligned(index, step, size):
    return pl.ds(pl.multiple_of(index * step, step), size)


def kernel(
    factor,
    x_ref, h_ref, g_ref, u_ref, wg_ref, wu_ref,
    dx_ref, dwg_ref, dwu_ref,
    g0, gbuf, wbuf, xt0, xbuf, dxs, dxr, dxp, dxq, dxo, dwt, dws, dwr, dwf,
    ga_s, ga_r, gr_s, gr_r, wa_s, wa_r, wc_s, wc_r, xa_s, xa_r, xb_s, xb_r, xc_s, xc_r,
    dy_s, dy_r, dq_s, dq_r, do_s, do_r, ec_s, ec_r, eo_s, eo_r,
):
    gx, gy, gz = lax.axis_index("gx"), lax.axis_index("gy"), lax.axis_index("gz")
    x, zh, y, zl, c = gy // NZH, gy % NZH, gz, gx // 2, gx % 2
    z = zh * NZL + zl
    rows = h_ref.shape[0]
    fq = h_ref.shape[1] // NX
    wr = wg_ref.shape[0]
    dc = 2 * wr
    shard = NX * rows
    blk = NZH * shard
    half = shard // 2
    w_refs, dw_refs = (wg_ref, wu_ref), (dwg_ref, dwu_ref)

    def dev(xx, yy, zz, cc):
        return ((zz % NZL) * 2 + cc, xx * NZH + zz // NZL, yy)

    def remote(src, dst, ss, rs, to):
        return pltpu.make_async_remote_copy(
            src_ref=src, dst_ref=dst, send_sem=ss, recv_sem=rs, device_id=to, device_id_type=MESH
        )

    here = dev(x, y, z, c)
    pair = dev(x, y, z, 1 - c)
    xs = [(x + k) % NX for k in range(NX)]
    ys = [(y + k) % NY for k in range(NY)]
    up, down = dev(x, y, (z + 1) % NZ, c), dev(x, y, (z + NZ - 1) % NZ, c)
    swapped = dev(x, zl, zh * NZL + y, c)
    on_diag = y == zl

    def landed(ref, sem):
        remote(ref, ref, sem, sem, pair).wait_recv()

    def sent(ref, sem):
        remote(ref, ref, sem, sem, pair).wait_send()

    barrier = pltpu.get_barrier_semaphore()

    def greet(to):
        pl.semaphore_signal(barrier, inc=1, device_id=to, device_id_type=MESH)

    for k in range(1, NX):
        greet(dev(xs[k], y, z, c))
    for k in range(1, NY):
        greet(dev(x, ys[k], z, c))
    greet(up)
    greet(down)
    greet(pair)

    for k in range(NY):

        @pl.when(jnp.logical_or(y != zl, y != k))
        def _():
            greet(dev(x, k, zh * NZL + y, c))

    greetings = (NX - 1) + (NY - 1) + 3 + NZL

    @pl.when(on_diag)
    def _():
        pl.semaphore_wait(barrier, greetings - 1)

    @pl.when(jnp.logical_not(on_diag))
    def _():
        pl.semaphore_wait(barrier, greetings)

    for q in range(NX):
        part = slice(q * fq, (q + 1) * fq)
        hh = h_ref[:, part].astype(F32)
        gg = g_ref[:, part].astype(F32)
        uu = u_ref[:, part].astype(F32)
        sq = jax.nn.sigmoid(gg)
        g0[q, 0] = (hh * uu * sq * (1.0 + gg * (1.0 - sq))).astype(BF16)
        g0[q, 1] = (hh * gg * sq).astype(BF16)

    def place(zz):
        zz = zz % NZ
        return (zz % NZL) * NZH + zz // NZL

    mine = place(z)
    g_mine = gbuf.at[:, mine, aligned(x, rows, rows), :]
    pltpu.make_async_copy(g0.at[x], g_mine, ga_r.at[x]).start()
    for k in range(1, NX):
        remote(g0.at[xs[k]], g_mine, ga_s.at[k], ga_r.at[x], dev(xs[k], y, z, c)).start()

    xin = x_ref[...].astype(F32)
    xp = jnp.concatenate(
        [xin[(i * NZH + j) * rows:(i * NZH + j + 1) * rows] for j in range(NZH) for i in range(NX)], axis=0
    )
    xt0[...] = xp.T.astype(BF16)
    x_dst = xbuf.at[aligned(x, dc, dc), aligned(zl, blk, blk)]

    @pl.when(on_diag)
    def _():
        pltpu.make_async_copy(xt0, x_dst, xa_r).start()

    @pl.when(jnp.logical_not(on_diag))
    def _():
        remote(xt0, x_dst, xa_s, xa_r, swapped).start()

    def w_src(gu, q):
        return w_refs[gu].at[:, aligned(q, fq, fq)]

    def w_rows(gu, i, cc):
        return wbuf.at[gu, aligned(i * 2 + cc, wr, wr), :]

    def w_send(gu, k):
        return remote(w_src(gu, xs[k]), w_rows(gu, x, c), wa_s.at[gu, k], wa_r.at[gu, x], dev(xs[k], y, z, c))

    def w_start(gu):
        pltpu.make_async_copy(w_src(gu, x), w_rows(gu, x, c), wa_r.at[gu, x]).start()
        for k in range(1, NX):
            w_send(gu, k).start()

    def w_forward(gu):
        for i in range(NX):
            landed(w_rows(gu, i, c), wa_r.at[gu, i])
            remote(w_rows(gu, i, c), w_rows(gu, i, c), wc_s.at[gu, i], wc_r.at[gu, i], pair).start()

    def ring_ref(gu, zz, part):
        return gbuf.at[gu, place(zz), pl.ds(part * half, half), :]

    def ring_send(gu, d, s, part):
        ref = ring_ref(gu, z + (NZ - s if d == 0 else s), part)
        return remote(ref, ref, gr_s.at[gu, d, s, part], gr_r.at[gu, d, s, part], up if d == 0 else down)

    def ring_landed(gu, d, s, part):
        landed(ring_ref(gu, z + (NZ - 1 - s if d == 0 else 1 + s), part), gr_r.at[gu, d, s, part])

    def part_of(d, j):
        return j if d == 0 else 1 - j

    last = NZ // 2 - 1

    def ring_first(gu):
        for j in range(2):
            for d in range(2):
                ring_send(gu, d, 0, part_of(d, j)).start()

    def ring_step(gu, s, j):
        for d in range(2):
            ring_landed(gu, d, s - 1, part_of(d, j))
            ring_send(gu, d, s, part_of(d, j)).start()

    def ring_near_end(gu):
        for d in range(2):
            ring_landed(gu, d, last - 1, part_of(d, 1))

    def ring_end(gu):
        for d in range(2):
            ring_landed(gu, d, last, part_of(d, 0))

    def x_piece(i, k):
        return xbuf.at[aligned(i, dc, dc), aligned(k, blk, blk)]

    def x_along_y(i):
        for k in range(1, NY):
            remote(x_piece(i, y), x_piece(i, y), xb_s.at[i, k], xb_r.at[i, y], dev(x, ys[k], z, c)).start()

    def x_start():
        landed(x_piece(x, y), xa_r)
        for k in range(1, NX):
            remote(x_piece(x, y), x_piece(x, y), xc_s.at[k], xc_r.at[x], dev(xs[k], y, z, c)).start()
        x_along_y(x)

    def x_forward():
        for k in range(1, NX):
            landed(x_piece(xs[k], y), xc_r.at[xs[k]])
            x_along_y(xs[k])

    def x_end():
        for i in range(NX):
            for k in range(1, NY):
                landed(x_piece(i, ys[k]), xb_r.at[i, ys[k]])

    def dw_out(gu, q):
        return dw_refs[gu].at[:, aligned(q, fq, fq)]

    def dw_send(gu, k):
        return remote(dwf.at[gu, xs[k]], dw_out(gu, x), eo_s.at[gu, k], eo_r.at[gu, x], dev(xs[k], y, z, c))

    def dw_pair(gu, i):
        return remote(dws.at[gu, i], dwr.at[gu, i], ec_s.at[gu, i], ec_r.at[gu, i], pair)

    def dw_compute(gu, first=0, end=NX):
        tokens = gbuf.at[gu]

        @pl.loop(first, end)
        def _(i):
            lhs = xbuf[aligned(i, dc, dc), :]
            rhs = tokens[...].reshape(NZ * shard, fq)
            dwt[gu, i] = jnp.dot(lhs, rhs, preferred_element_type=F32)
            dws[gu, i] = dwt[gu, i, aligned(1 - c, wr, wr), :].astype(BF16)
            dw_pair(gu, i).start()

    def dw_finish(gu):
        for k in range(NX - 1, -1, -1):
            i = xs[k]
            landed(dwr.at[gu, i], ec_r.at[gu, i])
            total = dwt[gu, i, aligned(c, wr, wr), :] + dwr[gu, i].astype(F32)
            dwf[gu, i] = (total * factor).astype(BF16)
            if k:
                dw_send(gu, k).start()
            else:
                pltpu.make_async_copy(dwf.at[gu, i], dw_out(gu, x), eo_r.at[gu, x]).start()

    def dx_rows(p, k):
        return dxs.at[p, aligned(k, rows, rows), :]

    def dx_shard(zz):
        zz = zz % NZ
        p = place(zz)

        @pl.loop(0, NX)
        def _(i):
            columns = aligned(i, dc, dc)
            total = lax.dot_general(
                gbuf[0, p], wbuf[0, columns, :], (((1,), (1,)), ((), ())), preferred_element_type=F32
            ) + lax.dot_general(
                gbuf[1, p], wbuf[1, columns, :], (((1,), (1,)), ((), ())), preferred_element_type=F32
            )
            dxs[p, :, columns] = total.astype(BF16)

        pltpu.make_async_copy(dx_rows(p, y), dxr.at[y, p], dy_r.at[p, y]).start()
        for k in range(1, NY):
            remote(dx_rows(p, ys[k]), dxr.at[y, p], dy_s.at[p, k], dy_r.at[p, y], dev(x, ys[k], z, c)).start()

    def w_end():
        for gu in range(2):
            for i in range(NX):
                landed(w_rows(gu, i, 1 - c), wc_r.at[gu, i])

    def dx_sum(*shards):
        for zz in shards:
            p = place(zz)
            for i in range(NY):
                landed(dxr.at[i, p], dy_r.at[p, i])
            total = dxr[0, p].astype(F32)
            for k in range(1, NY):
                total = total + dxr[k, p].astype(F32)
            for i in range(NX):
                dxp[i, p] = total[:, i * dc:(i + 1) * dc].astype(BF16)
            pltpu.make_async_copy(dxp.at[x, p], dxq.at[x, p], dq_r.at[p, x]).start()
            for k in range(1, NX):
                remote(dxp.at[xs[k], p], dxq.at[x, p], dq_s.at[p, k], dq_r.at[p, x], dev(xs[k], y, z, c)).start()

    def dx_out(*shards):
        for zz in shards:
            zz = zz % NZ
            p, j, owner = place(zz), zz // NZL, zz % NZL
            for i in range(NX):
                landed(dxq.at[i, p], dq_r.at[p, i])
            total = dxq[0, p].astype(F32)
            for k in range(1, NX):
                total = total + dxq[k, p].astype(F32)
            dxo[p] = total.astype(BF16)
            target = dx_ref.at[aligned(y * NZH + j, rows, rows), :]
            stays = jnp.logical_and(on_diag, owner == zl)

            @pl.when(stays)
            def _():
                pltpu.make_async_copy(dxo.at[p], target, do_r.at[y, j]).start()

            @pl.when(jnp.logical_not(stays))
            def _():
                remote(dxo.at[p], target, do_s.at[p], do_r.at[y, j], dev(x, zl, zh * NZL + owner, c)).start()

    def dx_end():
        for i in range(NY):
            for j in range(NZH):
                landed(dx_ref.at[pl.ds((i * NZH + j) * rows, rows), :], do_r.at[i, j])

    for i in range(NX):
        landed(gbuf.at[:, mine, pl.ds(i * rows, rows), :], ga_r.at[i])
    ring_first(0)
    x_start()
    w_start(0)
    ring_step(0, 1, 0)
    x_forward()
    ring_step(0, 1, 1)
    w_start(1)
    ring_step(0, 2, 0)
    w_forward(0)
    ring_step(0, 2, 1)
    ring_step(0, 3, 0)
    ring_first(1)
    ring_near_end(0)
    ring_end(0)
    ring_step(1, 1, 0)
    ring_step(1, 1, 1)
    w_forward(1)
    x_end()
    dw_compute(0)
    ring_step(1, 2, 0)
    w_end()
    dx_shard(z)
    dw_finish(0)
    ring_step(1, 2, 1)
    dx_shard(z + NZ - 1)
    dx_shard(z + 1)
    ring_step(1, 3, 0)
    dx_shard(z + NZ - 2)
    dx_shard(z + 2)
    ring_near_end(1)
    dx_shard(z + NZ - 3)
    dx_shard(z + 3)
    dx_sum(z, z + NZ - 1, z + 1, z + NZ - 2, z + 2)
    ring_end(1)
    dx_shard(z + 4)
    dw_compute(1)
    dx_sum(z + NZ - 3, z + 3, z + 4)
    dx_out(z, z + NZ - 1, z + 1, z + NZ - 2, z + 2)
    dw_finish(1)
    dx_out(z + NZ - 3, z + 3, z + 4)
    dx_end()

    for gu in range(2):
        for i in range(NX):
            landed(dw_out(gu, i), eo_r.at[gu, i])
    for k in range(1, NX):
        sent(g0.at[xs[k]], ga_s.at[k])
        sent(x_piece(x, y), xc_s.at[k])
        for i in range(NX):
            sent(x_piece(i, y), xb_s.at[i, k])
        for p in range(NZ):
            sent(dx_rows(p, ys[k]), dy_s.at[p, k])
            sent(dxp.at[xs[k], p], dq_s.at[p, k])
        for gu in range(2):
            sent(w_src(gu, xs[k]), wa_s.at[gu, k])
            sent(dwf.at[gu, xs[k]], eo_s.at[gu, k])

    @pl.when(jnp.logical_not(on_diag))
    def _():
        sent(xt0, xa_s)

    for gu in range(2):
        for i in range(NX):
            sent(w_rows(gu, i, c), wc_s.at[gu, i])
            sent(dws.at[gu, i], ec_s.at[gu, i])
        for s in range(last + 1):
            for j in range(2 if s < last else 1):
                for d in range(2):
                    ring_send(gu, d, s, part_of(d, j)).wait_send()
    for p in range(NZ):

        @pl.when(jnp.logical_not(jnp.logical_and(on_diag, p // NZH == zl)))
        def _():
            sent(dxo.at[p], do_s.at[p])


def body(inputs, hidden_grad, gate_pre, up_pre, gate_weight, up_weight):
    rows, width = hidden_grad.shape
    wr = gate_weight.shape[0]
    fq, shard, dc = width // NX, NX * rows, 2 * wr
    tokens, columns = NZ * shard, NX * dc
    factor = 1.0 / math.sqrt(inputs.shape[0] * lax.axis_size("gx"))
    vmem, anywhere = pl.BlockSpec(memory_space=pltpu.VMEM), pl.BlockSpec(memory_space=pl.ANY)
    dma = pltpu.SemaphoreType.DMA
    return pl.pallas_call(
        functools.partial(kernel, factor),
        out_shape=(
            jax.ShapeDtypeStruct(inputs.shape, BF16),
            jax.ShapeDtypeStruct(gate_weight.shape, BF16),
            jax.ShapeDtypeStruct(up_weight.shape, BF16),
        ),
        in_specs=[vmem, vmem, vmem, vmem, anywhere, anywhere],
        out_specs=(vmem, anywhere, anywhere),
        scratch_shapes=[
            pltpu.VMEM((NX, 2, rows, fq), BF16),
            pltpu.VMEM((2, NZ, shard, fq), BF16),
            pltpu.VMEM((2, columns, fq), BF16),
            pltpu.VMEM((dc, NZH * shard), BF16),
            pltpu.VMEM((columns, tokens), BF16),
            pltpu.VMEM((NZ, shard, columns), BF16),
            pltpu.VMEM((NY, NZ, rows, columns), BF16),
            pltpu.VMEM((NX, NZ, rows, dc), BF16),
            pltpu.VMEM((NX, NZ, rows, dc), BF16),
            pltpu.VMEM((NZ, rows, dc), BF16),
            pltpu.VMEM((2, NX, dc, fq), F32),
            pltpu.VMEM((2, NX, wr, fq), BF16),
            pltpu.VMEM((2, NX, wr, fq), BF16),
            pltpu.VMEM((2, NX, wr, fq), BF16),
            dma((NX,)), dma((NX,)),
            dma((2, 2, NZ // 2, 2)), dma((2, 2, NZ // 2, 2)),
            dma((2, NX)), dma((2, NX)),
            dma((2, NX)), dma((2, NX)),
            dma, dma,
            dma((NX, NY)), dma((NX, NY)),
            dma((NX,)), dma((NX,)),
            dma((NZ, NY)), dma((NZ, NY)),
            dma((NZ, NX)), dma((NZ, NX)),
            dma((NZ,)), dma((NY, NZH)),
            dma((2, NX)), dma((2, NX)),
            dma((2, NX)), dma((2, NX)),
        ],
        compiler_params=pltpu.CompilerParams(
            collective_id=0, has_side_effects=True, vmem_limit_bytes=56 << 20
        ),
        cost_estimate=pl.CostEstimate(
            flops=8 * tokens * columns * fq, bytes_accessed=12 * wr * width, transcendentals=rows * width
        ),
        name="swiglu_backward",
    )(inputs, hidden_grad, gate_pre, up_pre, gate_weight, up_weight)


def solution(mesh):
    placed = (
        P("gx", ("gy", "gz")),
        P(("gx", "gy"), "gz"),
        P(("gx", "gy"), "gz"),
        P(("gx", "gy"), "gz"),
        P(("gy", "gx"), "gz"),
        P(("gy", "gx"), "gz"),
    )
    return jax.shard_map(
        body,
        mesh=mesh,
        in_specs=placed,
        out_specs=(P("gx", ("gy", "gz")), P(("gy", "gx"), "gz"), P(("gy", "gx"), "gz")),
        check_vma=False,
    )
```

```python
import functools
import math

import jax
import jax.numpy as jnp
from jax import lax
from jax.experimental import pallas as pl
from jax.experimental.pallas import tpu as pltpu
from jax.sharding import PartitionSpec as P

MESH = pl.DeviceIdType.MESH
BF16, F32 = jnp.bfloat16, jnp.float32

NX, NY, NZH, NZL = 4, 4, 2, 4
NZ = NZH * NZL


def aligned(index, step, size):
    return pl.ds(pl.multiple_of(index * step, step), size)


def kernel(
    factor,
    x_ref, h_ref, g_ref, u_ref, wg_ref, wu_ref,
    dx_ref, dwg_ref, dwu_ref,
    g0, gbuf, wbuf, xt0, xbuf, dxs, dxr, dxp, dxq, dxo, dwt, dws, dwr, dwf,
    ga_s, ga_r, gr_s, gr_r, wa_s, wa_r, wc_s, wc_r, xa_s, xa_r, xb_s, xb_r, xc_s, xc_r,
    dy_s, dy_r, dq_s, dq_r, do_s, do_r, ec_s, ec_r, eo_s, eo_r,
):
    gx, gy, gz = lax.axis_index("gx"), lax.axis_index("gy"), lax.axis_index("gz")
    x, zh, y, zl, c = gy // NZH, gy % NZH, gz, gx // 2, gx % 2
    z = zh * NZL + zl
    rows = h_ref.shape[0]
    fq = h_ref.shape[1] // NX
    wr = wg_ref.shape[0]
    dc = 2 * wr
    shard = NX * rows
    blk = NZH * shard
    half = shard // 2
    w_refs, dw_refs = (wg_ref, wu_ref), (dwg_ref, dwu_ref)

    def dev(xx, yy, zz, cc):
        return ((zz % NZL) * 2 + cc, xx * NZH + zz // NZL, yy)

    def remote(src, dst, ss, rs, to):
        return pltpu.make_async_remote_copy(
            src_ref=src, dst_ref=dst, send_sem=ss, recv_sem=rs, device_id=to, device_id_type=MESH
        )

    here = dev(x, y, z, c)
    pair = dev(x, y, z, 1 - c)
    xs = [(x + k) % NX for k in range(NX)]
    ys = [(y + k) % NY for k in range(NY)]
    up, down = dev(x, y, (z + 1) % NZ, c), dev(x, y, (z + NZ - 1) % NZ, c)
    swapped = dev(x, zl, zh * NZL + y, c)
    on_diag = y == zl

    def landed(ref, sem):
        remote(ref, ref, sem, sem, pair).wait_recv()

    def sent(ref, sem):
        remote(ref, ref, sem, sem, pair).wait_send()

    barrier = pltpu.get_barrier_semaphore()

    def greet(to):
        pl.semaphore_signal(barrier, inc=1, device_id=to, device_id_type=MESH)

    for k in range(1, NX):
        greet(dev(xs[k], y, z, c))
    for k in range(1, NY):
        greet(dev(x, ys[k], z, c))
    greet(up)
    greet(down)
    greet(pair)

    for k in range(NY):

        @pl.when(jnp.logical_or(y != zl, y != k))
        def _():
            greet(dev(x, k, zh * NZL + y, c))

    greetings = (NX - 1) + (NY - 1) + 3 + NZL

    @pl.when(on_diag)
    def _():
        pl.semaphore_wait(barrier, greetings - 1)

    @pl.when(jnp.logical_not(on_diag))
    def _():
        pl.semaphore_wait(barrier, greetings)

    for q in range(NX):
        part = slice(q * fq, (q + 1) * fq)
        hh = h_ref[:, part].astype(F32)
        gg = g_ref[:, part].astype(F32)
        uu = u_ref[:, part].astype(F32)
        sq = jax.nn.sigmoid(gg)
        g0[q, 0] = (hh * uu * sq * (1.0 + gg * (1.0 - sq))).astype(BF16)
        g0[q, 1] = (hh * gg * sq).astype(BF16)

    def place(zz):
        zz = zz % NZ
        return (zz % NZL) * NZH + zz // NZL

    mine = place(z)
    g_mine = gbuf.at[:, mine, aligned(x, rows, rows), :]
    pltpu.make_async_copy(g0.at[x], g_mine, ga_r.at[x]).start()
    for k in range(1, NX):
        remote(g0.at[xs[k]], g_mine, ga_s.at[k], ga_r.at[x], dev(xs[k], y, z, c)).start()

    xin = x_ref[...].astype(F32)
    xp = jnp.concatenate(
        [xin[(i * NZH + j) * rows:(i * NZH + j + 1) * rows] for j in range(NZH) for i in range(NX)], axis=0
    )
    xt0[...] = xp.T.astype(BF16)
    x_dst = xbuf.at[aligned(x, dc, dc), aligned(zl, blk, blk)]

    @pl.when(on_diag)
    def _():
        pltpu.make_async_copy(xt0, x_dst, xa_r).start()

    @pl.when(jnp.logical_not(on_diag))
    def _():
        remote(xt0, x_dst, xa_s, xa_r, swapped).start()

    def w_src(gu, q):
        return w_refs[gu].at[:, aligned(q, fq, fq)]

    def w_rows(gu, i, cc):
        return wbuf.at[gu, aligned(i * 2 + cc, wr, wr), :]

    def w_send(gu, k):
        return remote(w_src(gu, xs[k]), w_rows(gu, x, c), wa_s.at[gu, k], wa_r.at[gu, x], dev(xs[k], y, z, c))

    def w_start(gu):
        pltpu.make_async_copy(w_src(gu, x), w_rows(gu, x, c), wa_r.at[gu, x]).start()
        for k in range(1, NX):
            w_send(gu, k).start()

    def w_forward(gu):
        for i in range(NX):
            landed(w_rows(gu, i, c), wa_r.at[gu, i])
            remote(w_rows(gu, i, c), w_rows(gu, i, c), wc_s.at[gu, i], wc_r.at[gu, i], pair).start()

    def ring_ref(gu, zz, part):
        return gbuf.at[gu, place(zz), pl.ds(part * half, half), :]

    def ring_send(gu, d, s, part):
        ref = ring_ref(gu, z + (NZ - s if d == 0 else s), part)
        return remote(ref, ref, gr_s.at[gu, d, s, part], gr_r.at[gu, d, s, part], up if d == 0 else down)

    def ring_landed(gu, d, s, part):
        landed(ring_ref(gu, z + (NZ - 1 - s if d == 0 else 1 + s), part), gr_r.at[gu, d, s, part])

    def part_of(d, j):
        return j if d == 0 else 1 - j

    last = NZ // 2 - 1

    def ring_first(gu):
        for j in range(2):
            for d in range(2):
                ring_send(gu, d, 0, part_of(d, j)).start()

    def ring_step(gu, s, j):
        for d in range(2):
            ring_landed(gu, d, s - 1, part_of(d, j))
            ring_send(gu, d, s, part_of(d, j)).start()

    def ring_near_end(gu):
        for d in range(2):
            ring_landed(gu, d, last - 1, part_of(d, 1))

    def ring_end(gu):
        for d in range(2):
            ring_landed(gu, d, last, part_of(d, 0))

    def x_piece(i, k):
        return xbuf.at[aligned(i, dc, dc), aligned(k, blk, blk)]

    def x_along_y(i):
        for k in range(1, NY):
            remote(x_piece(i, y), x_piece(i, y), xb_s.at[i, k], xb_r.at[i, y], dev(x, ys[k], z, c)).start()

    def x_start():
        landed(x_piece(x, y), xa_r)
        for k in range(1, NX):
            remote(x_piece(x, y), x_piece(x, y), xc_s.at[k], xc_r.at[x], dev(xs[k], y, z, c)).start()
        x_along_y(x)

    def x_forward():
        for k in range(1, NX):
            landed(x_piece(xs[k], y), xc_r.at[xs[k]])
            x_along_y(xs[k])

    def x_end():
        for i in range(NX):
            for k in range(1, NY):
                landed(x_piece(i, ys[k]), xb_r.at[i, ys[k]])

    def dw_out(gu, q):
        return dw_refs[gu].at[:, aligned(q, fq, fq)]

    def dw_send(gu, k):
        return remote(dwf.at[gu, xs[k]], dw_out(gu, x), eo_s.at[gu, k], eo_r.at[gu, x], dev(xs[k], y, z, c))

    def dw_pair(gu, i):
        return remote(dws.at[gu, i], dwr.at[gu, i], ec_s.at[gu, i], ec_r.at[gu, i], pair)

    def dw_compute(gu, first=0, end=NX):
        tokens = gbuf.at[gu]

        @pl.loop(first, end)
        def _(i):
            lhs = xbuf[aligned(i, dc, dc), :]
            rhs = tokens[...].reshape(NZ * shard, fq)
            dwt[gu, i] = jnp.dot(lhs, rhs, preferred_element_type=F32)
            dws[gu, i] = dwt[gu, i, aligned(1 - c, wr, wr), :].astype(BF16)
            dw_pair(gu, i).start()

    def dw_finish(gu):
        for k in range(NX - 1, -1, -1):
            i = xs[k]
            landed(dwr.at[gu, i], ec_r.at[gu, i])
            total = dwt[gu, i, aligned(c, wr, wr), :] + dwr[gu, i].astype(F32)
            dwf[gu, i] = (total * factor).astype(BF16)
            if k:
                dw_send(gu, k).start()
            else:
                pltpu.make_async_copy(dwf.at[gu, i], dw_out(gu, x), eo_r.at[gu, x]).start()

    def dx_rows(p, k):
        return dxs.at[p, aligned(k, rows, rows), :]

    def dx_shard(zz):
        zz = zz % NZ
        p = place(zz)

        @pl.loop(0, NX)
        def _(i):
            columns = aligned(i, dc, dc)
            total = lax.dot_general(
                gbuf[0, p], wbuf[0, columns, :], (((1,), (1,)), ((), ())), preferred_element_type=F32
            ) + lax.dot_general(
                gbuf[1, p], wbuf[1, columns, :], (((1,), (1,)), ((), ())), preferred_element_type=F32
            )
            dxs[p, :, columns] = total.astype(BF16)

        pltpu.make_async_copy(dx_rows(p, y), dxr.at[y, p], dy_r.at[p, y]).start()
        for k in range(1, NY):
            remote(dx_rows(p, ys[k]), dxr.at[y, p], dy_s.at[p, k], dy_r.at[p, y], dev(x, ys[k], z, c)).start()

    def w_end():
        for gu in range(2):
            for i in range(NX):
                landed(w_rows(gu, i, 1 - c), wc_r.at[gu, i])

    def dx_sum(*shards):
        for zz in shards:
            p = place(zz)
            for i in range(NY):
                landed(dxr.at[i, p], dy_r.at[p, i])
            total = dxr[0, p].astype(F32)
            for k in range(1, NY):
                total = total + dxr[k, p].astype(F32)
            for i in range(NX):
                dxp[i, p] = total[:, i * dc:(i + 1) * dc].astype(BF16)
            pltpu.make_async_copy(dxp.at[x, p], dxq.at[x, p], dq_r.at[p, x]).start()
            for k in range(1, NX):
                remote(dxp.at[xs[k], p], dxq.at[x, p], dq_s.at[p, k], dq_r.at[p, x], dev(xs[k], y, z, c)).start()

    def dx_out(*shards):
        for zz in shards:
            zz = zz % NZ
            p, j, owner = place(zz), zz // NZL, zz % NZL
            for i in range(NX):
                landed(dxq.at[i, p], dq_r.at[p, i])
            total = dxq[0, p].astype(F32)
            for k in range(1, NX):
                total = total + dxq[k, p].astype(F32)
            dxo[p] = total.astype(BF16)
            target = dx_ref.at[aligned(y * NZH + j, rows, rows), :]
            stays = jnp.logical_and(on_diag, owner == zl)

            @pl.when(stays)
            def _():
                pltpu.make_async_copy(dxo.at[p], target, do_r.at[y, j]).start()

            @pl.when(jnp.logical_not(stays))
            def _():
                remote(dxo.at[p], target, do_s.at[p], do_r.at[y, j], dev(x, zl, zh * NZL + owner, c)).start()

    def dx_end():
        for i in range(NY):
            for j in range(NZH):
                landed(dx_ref.at[pl.ds((i * NZH + j) * rows, rows), :], do_r.at[i, j])

    for i in range(NX):
        landed(gbuf.at[:, mine, pl.ds(i * rows, rows), :], ga_r.at[i])
    ring_first(0)
    w_start(0)
    x_start()
    ring_step(0, 1, 0)
    ring_step(0, 1, 1)
    x_forward()
    w_start(1)
    ring_step(0, 2, 0)
    w_forward(0)
    ring_step(0, 2, 1)
    ring_step(0, 3, 0)
    ring_first(1)
    ring_near_end(0)
    ring_end(0)
    ring_step(1, 1, 0)
    ring_step(1, 1, 1)
    w_forward(1)
    x_end()
    dw_compute(0)
    ring_step(1, 2, 0)
    w_end()
    dx_shard(z)
    dw_finish(0)
    ring_step(1, 2, 1)
    dx_shard(z + NZ - 1)
    dx_shard(z + 1)
    ring_step(1, 3, 0)
    dx_shard(z + NZ - 2)
    dx_shard(z + 2)
    ring_near_end(1)
    dx_shard(z + NZ - 3)
    dx_shard(z + 3)
    ring_end(1)
    dx_shard(z + 4)
    dx_sum(z, z + NZ - 1, z + 1, z + NZ - 2, z + 2)
    dw_compute(1)
    dx_sum(z + NZ - 3, z + 3, z + 4)
    dx_out(z, z + NZ - 1, z + 1, z + NZ - 2, z + 2)
    dw_finish(1)
    dx_out(z + NZ - 3, z + 3, z + 4)
    dx_end()

    for gu in range(2):
        for i in range(NX):
            landed(dw_out(gu, i), eo_r.at[gu, i])
    for k in range(1, NX):
        sent(g0.at[xs[k]], ga_s.at[k])
        sent(x_piece(x, y), xc_s.at[k])
        for i in range(NX):
            sent(x_piece(i, y), xb_s.at[i, k])
        for p in range(NZ):
            sent(dx_rows(p, ys[k]), dy_s.at[p, k])
            sent(dxp.at[xs[k], p], dq_s.at[p, k])
        for gu in range(2):
            sent(w_src(gu, xs[k]), wa_s.at[gu, k])
            sent(dwf.at[gu, xs[k]], eo_s.at[gu, k])

    @pl.when(jnp.logical_not(on_diag))
    def _():
        sent(xt0, xa_s)

    for gu in range(2):
        for i in range(NX):
            sent(w_rows(gu, i, c), wc_s.at[gu, i])
            sent(dws.at[gu, i], ec_s.at[gu, i])
        for s in range(last + 1):
            for j in range(2 if s < last else 1):
                for d in range(2):
                    ring_send(gu, d, s, part_of(d, j)).wait_send()
    for p in range(NZ):

        @pl.when(jnp.logical_not(jnp.logical_and(on_diag, p // NZH == zl)))
        def _():
            sent(dxo.at[p], do_s.at[p])


def body(inputs, hidden_grad, gate_pre, up_pre, gate_weight, up_weight):
    rows, width = hidden_grad.shape
    wr = gate_weight.shape[0]
    fq, shard, dc = width // NX, NX * rows, 2 * wr
    tokens, columns = NZ * shard, NX * dc
    factor = 1.0 / math.sqrt(inputs.shape[0] * lax.axis_size("gx"))
    vmem, anywhere = pl.BlockSpec(memory_space=pltpu.VMEM), pl.BlockSpec(memory_space=pl.ANY)
    dma = pltpu.SemaphoreType.DMA
    return pl.pallas_call(
        functools.partial(kernel, factor),
        out_shape=(
            jax.ShapeDtypeStruct(inputs.shape, BF16),
            jax.ShapeDtypeStruct(gate_weight.shape, BF16),
            jax.ShapeDtypeStruct(up_weight.shape, BF16),
        ),
        in_specs=[vmem, vmem, vmem, vmem, anywhere, anywhere],
        out_specs=(vmem, anywhere, anywhere),
        scratch_shapes=[
            pltpu.VMEM((NX, 2, rows, fq), BF16),
            pltpu.VMEM((2, NZ, shard, fq), BF16),
            pltpu.VMEM((2, columns, fq), BF16),
            pltpu.VMEM((dc, NZH * shard), BF16),
            pltpu.VMEM((columns, tokens), BF16),
            pltpu.VMEM((NZ, shard, columns), BF16),
            pltpu.VMEM((NY, NZ, rows, columns), BF16),
            pltpu.VMEM((NX, NZ, rows, dc), BF16),
            pltpu.VMEM((NX, NZ, rows, dc), BF16),
            pltpu.VMEM((NZ, rows, dc), BF16),
            pltpu.VMEM((2, NX, dc, fq), F32),
            pltpu.VMEM((2, NX, wr, fq), BF16),
            pltpu.VMEM((2, NX, wr, fq), BF16),
            pltpu.VMEM((2, NX, wr, fq), BF16),
            dma((NX,)), dma((NX,)),
            dma((2, 2, NZ // 2, 2)), dma((2, 2, NZ // 2, 2)),
            dma((2, NX)), dma((2, NX)),
            dma((2, NX)), dma((2, NX)),
            dma, dma,
            dma((NX, NY)), dma((NX, NY)),
            dma((NX,)), dma((NX,)),
            dma((NZ, NY)), dma((NZ, NY)),
            dma((NZ, NX)), dma((NZ, NX)),
            dma((NZ,)), dma((NY, NZH)),
            dma((2, NX)), dma((2, NX)),
            dma((2, NX)), dma((2, NX)),
        ],
        compiler_params=pltpu.CompilerParams(
            collective_id=0, has_side_effects=True, vmem_limit_bytes=56 << 20
        ),
        cost_estimate=pl.CostEstimate(
            flops=8 * tokens * columns * fq, bytes_accessed=12 * wr * width, transcendentals=rows * width
        ),
        name="swiglu_backward",
    )(inputs, hidden_grad, gate_pre, up_pre, gate_weight, up_weight)


def solution(mesh):
    placed = (
        P("gx", ("gy", "gz")),
        P(("gx", "gy"), "gz"),
        P(("gx", "gy"), "gz"),
        P(("gx", "gy"), "gz"),
        P(("gy", "gx"), "gz"),
        P(("gy", "gx"), "gz"),
    )
    return jax.shard_map(
        body,
        mesh=mesh,
        in_specs=placed,
        out_specs=(P("gx", ("gy", "gz")), P(("gy", "gx"), "gz"), P(("gy", "gx"), "gz")),
        check_vma=False,
    )
```
